32 devices in a mesh: groups: 2 (over y), tok: 16 (over z, x, core).
Axes of the slice: x: 2, y: 2, z: 4, core: 2. Of those that a mesh axis runs over, the one named last changes fastest.
Arguments:
- activations: bfloat16 [2, 20480, 2048], P(None, ('groups', 'tok')), parts along dimension 1, may hold values from -6 to 6
- gradients: bfloat16 [2, 20480, 2048], P(None, ('groups', 'tok')), parts along dimension 1, may hold values from -6 to 6
- query_u: bfloat16 [4, 2048, 1024], P('groups', 'tok'), parts along dimension 0, may hold values from -4 to 4
- query_v: bfloat16 [4, 2048, 1024], P('groups', 'tok'), parts along dimension 0, may hold values from -4 to 4
- block_ids: int32 [4, 16], P('groups'), parts along dimension 0, may hold values from 0 to 31
- counts: int32 [32], P(('groups', 'tok')), parts along dimension 0, may hold values from 1 to 640, 5440 in all
Outputs:
- scores: float32 [20480, 64], P(('groups', 'tok')), parts along dimension 0
The draws below stay inside these ranges and needn't reach their ends.
There are 2 independent parts, one for each index of `groups`. The reference program is written for one: setup_inputs(seed, part) draws one part's arguments, and reference() takes and returns one part's arrays. A program takes and returns all parts, laid end to end along the dimension named above; each array names one. Nothing has to cross between parts.
Inputs may be any that keep to these rules, and one draw needn't show every extreme that they name: The counts of one part sum to (16 + 1) * 320 and the largest equals 640.
All inputs are finite; a program needn't handle non-finite values. No bound on the sum of `counts` on one device may be relied on, other than what follows from the above.
Results may differ from the reference program's by a relative error of at most 0.0003.
Values may be sent and summed in bfloat16 or wider, within the bound.
A program may use at most 64 MiB of HBM per device.

```python
import math
import jax
import jax.numpy as jnp
import numpy as np
from jax import lax

D = 2048
LAYERS = 2
RANK = 8
QB = 4
NB = 16
BANK = 32
TOK_DEV = 640
NQ = 64
TOKENS = 10240
N_TOK = 16


def factor_drawn(key):
    keys = jax.random.split(key, 3)
    groups = BANK * QB
    common = jnp.clip(jax.random.normal(keys[0], (LAYERS, D, groups, 1), jnp.float32), -6.0, 6.0)
    own = jnp.clip(jax.random.normal(keys[1], (LAYERS, D, groups, RANK), jnp.float32), -6.0, 6.0)
    mixing = jax.random.uniform(keys[2], (LAYERS, 1, groups, 1), jnp.float32, 0.25, 0.6)
    values = (jnp.sqrt(mixing) * common + jnp.sqrt(1.0 - mixing) * own) * D ** (-0.5)
    return values.reshape(LAYERS, D, groups * RANK).astype(jnp.bfloat16)


def draw_query_u(key, part):
    inner = jax.random.fold_in(key, 11)
    return factor_drawn(inner)


def draw_query_v(key, part):
    inner = jax.random.fold_in(key, 23)
    return factor_drawn(inner)


def plant(values, rng, low, top_value):
    longest = values.shape.index(max(values.shape))
    spots = []
    for shift in (0, 1):
        where = [jax.random.randint(jax.random.fold_in(rng, axis), (), 0, length) for axis, length in enumerate(values.shape)]
        where[longest] = (where[longest] + shift) % values.shape[longest]
        spots.append(tuple(where))
    return values.at[spots[0]].set(low).at[spots[1]].set(top_value)


def level_of(stream_key, extent, cuts, smallest, high):
    level, own = 1.0, jax.random.fold_in(stream_key, 6)
    for position, parts in cuts:
        steps = jnp.exp(jax.random.uniform(jax.random.fold_in(own, position), (parts,), jnp.float32, smallest / len(cuts), high / len(cuts)))
        level = level * jnp.repeat(steps, extent[position] // parts).reshape([-1 if axis == position else 1 for axis in range(len(extent))])
    return level


def length_profile(amount, total, reach, skew):
    weights = [(1 << 20) // math.isqrt(standing ** skew) + 1 for standing in range(2, amount + 1)]
    spare, given = total - reach - (amount - 1), [1] * (amount - 1)
    while spare > 0:
        free = [i for i in range(amount - 1) if given[i] < reach]
        pool, budget = sum([weights[i] for i in free]), spare
        for i in free:
            addition = min(reach - given[i], max(1, budget * weights[i] // pool), spare)
            given[i] = given[i] + addition
            spare = spare - addition
    return np.array([reach] + given)


def uneven(key, count, total, limit, lean):
    if count == 2:
        one = jax.random.randint(key, (), max(1, total - limit), min(limit, total - 1) + 1)
        return jnp.stack([one, total - one])
    lengths = jnp.asarray(length_profile(count, total, limit, lean), jnp.int32)
    pairs = (count - 1) // 2
    giver, taker = lengths[1:1 + 2 * pairs:2], lengths[2:2 + 2 * pairs:2]
    margin = jnp.minimum(giver - 1, limit - taker)
    moved = jax.random.randint(jax.random.fold_in(key, 1), (pairs,), 0, 1 << 20) % (margin + 1)
    lengths = lengths.at[1:1 + 2 * pairs:2].set(giver - moved).at[2:2 + 2 * pairs:2].set(taker + moved)
    return lengths[jax.random.permutation(jax.random.fold_in(key, 2), count)]


def scatter_about(own_key, dims, spread, most, cuts=(), kind=jnp.bfloat16):
    gain = level_of(own_key, dims, cuts, -0.22, 0.18) if cuts else 1.0
    entries = jax.random.normal(own_key, dims, jnp.float32) * spread * gain
    return jnp.minimum(jnp.maximum(entries, -most), most).astype(kind)


def setup_inputs(seed: int = 0, part: int = 0) -> dict:
    seeds = jax.random.split(jax.random.key(seed), 7)
    own_keys = jax.random.split(jax.random.fold_in(seeds[6], part), 7)
    return {
        "activations": scatter_about(own_keys[0], (LAYERS, TOKENS, D), 1.0, 6.0, ((1, 16),)),
        "gradients": scatter_about(own_keys[1], (LAYERS, TOKENS, D), 1.0, 6.0, ((1, 16),)),
        "query_u": draw_query_u(jax.random.fold_in(jax.random.fold_in(seeds[6], part), 71), part),
        "query_v": draw_query_v(jax.random.fold_in(jax.random.fold_in(seeds[6], part), 71), part),
        "block_ids": plant(jax.random.randint(own_keys[4], (LAYERS, NB), 0, BANK), jax.random.fold_in(own_keys[4], 1), 0, BANK - 1).astype(jnp.int32),
        "counts": uneven(own_keys[5], N_TOK, (N_TOK + 1) * TOK_DEV // 2, TOK_DEV, 2).astype(jnp.int32),
    }


def pick_columns(factor, block_ids):
    width = QB * RANK
    chosen = []
    for layer in range(factor.shape[0]):
        slots = factor[layer].reshape(factor.shape[1], -1, width)
        chosen.append(jnp.take(slots, block_ids[layer].astype(jnp.int32), axis=1).reshape(factor.shape[1], -1))
    return jnp.stack(chosen)

def rank_grams(factor):
    per = factor.astype(jnp.float32).reshape(factor.shape[0], factor.shape[1], -1, RANK)
    return jnp.einsum('lkqr,lkqs->lqrs', per, per)

def reference(activations, gradients, query_u, query_v, block_ids, counts):
    chosen_u = pick_columns(query_u, block_ids)
    chosen_v = pick_columns(query_v, block_ids)
    raw = jnp.zeros((TOKENS, NQ), jnp.float32)
    for layer in range(LAYERS):
        grad_proj = jnp.dot(gradients[layer], chosen_u[layer], preferred_element_type=jnp.float32)
        act_proj = jnp.dot(activations[layer], chosen_v[layer], preferred_element_type=jnp.float32)
        raw = raw + lax.optimization_barrier(jnp.sum((grad_proj * act_proj).reshape(TOKENS, NQ, RANK), axis=2))
    norm_sq = lax.optimization_barrier(jnp.sum(rank_grams(chosen_u) * rank_grams(chosen_v), axis=(0, 2, 3)))
    slot = jnp.arange(TOKENS, dtype=jnp.int32)
    owner = slot // TOK_DEV
    live = slot % TOK_DEV < counts[owner]
    scaled = raw / jnp.sqrt(norm_sq + 1e-06)[None, :]
    return jnp.where(live[:, None], scaled, jnp.zeros_like(scaled))
```

```python
import functools

import jax
import jax.numpy as jnp
from jax import lax
from jax.experimental import pallas as pl
from jax.experimental.pallas import tpu as pltpu
from jax.sharding import PartitionSpec as P

RANK = 8
QB = 4
WIDTH = QB * RANK
Z = 4
X = 2
CORES = 2
CHIPS = Z * X
HALF = 256
AROUND = 1
MESH = pl.DeviceIdType.MESH


def column_names(block_ids):
    within = jnp.arange(block_ids.shape[1] * WIDTH, dtype=jnp.int32) % WIDTH
    return jnp.repeat(block_ids, WIDTH, axis=1) * WIDTH + within[None, :]


def pick_columns(factor, names):
    rows = jnp.arange(factor.shape[2], dtype=jnp.int32)
    pick = (rows[None, :, None] == names[:, None, :]).astype(factor.dtype)
    chosen = jnp.einsum("lkn,lnc->lkc", factor, pick, preferred_element_type=jnp.float32)
    return chosen.astype(factor.dtype)


def rank_grams(factor):
    per = factor.reshape(factor.shape[0], factor.shape[1], -1, RANK)
    return jnp.einsum("lkqr,lkqs->lqrs", per, per, preferred_element_type=jnp.float32)


def gathered(activations, gradients, query_u, query_v, block_ids):
    layers, tok_rows, _ = activations.shape
    queries = block_ids.shape[1] * QB
    names = column_names(block_ids)
    whole_u = lax.all_gather(pick_columns(query_u, names), "tok", axis=1, tiled=True)
    whole_v = lax.all_gather(pick_columns(query_v, names), "tok", axis=1, tiled=True)
    grad_proj = jnp.einsum("ltk,lkc->ltc", gradients, whole_u, preferred_element_type=jnp.float32)
    act_proj = jnp.einsum("ltk,lkc->ltc", activations, whole_v, preferred_element_type=jnp.float32)
    raw = jnp.sum((grad_proj * act_proj).reshape(layers, tok_rows, queries, RANK), axis=(0, 3))
    norm_sq = jnp.sum(rank_grams(whole_u) * rank_grams(whole_v), axis=(0, 2, 3))
    return raw / jnp.sqrt(norm_sq + 1e-06)[None, :]


def split_dot(value, ones, parts):
    total = None
    for _ in range(parts):
        head = value.astype(jnp.bfloat16)
        term = jnp.dot(head, ones, preferred_element_type=jnp.float32)
        total = term if total is None else total + term
        value = value - head.astype(jnp.float32)
    return total


def kernel(layers, halves, act_ref, grad_ref, qu_ref, qv_ref, col_ref, out_ref,
           whole, toks, acc, gram, tok_sem, send_sem, recv_sem):
    pieces = layers * halves * 2
    shard = qu_ref.shape[1]
    bank = qu_ref.shape[2]
    depth = CORES * shard
    me = lax.axis_index("tok")
    c = lax.rem(me, CORES)
    x = lax.rem(me // CORES, X)
    z = me // (CORES * X)

    def device(zz, xx, cc):
        return (zz * X + xx) * CORES + cc

    targets = (
        device(lax.rem(z + 1, Z), x, c),
        device(lax.rem(z + Z - 1, Z), x, c),
        device(z, 1 - x, c),
        device(z, x, 1 - c),
    )

    loads = []
    for layer in range(layers):
        for side, ref in enumerate((grad_ref, act_ref)):
            m = layer * 2 + side
            loads.append(pltpu.make_async_copy(ref.at[layer], toks.at[m], tok_sem.at[m]))
    for load in loads:
        load.start()

    barrier = pltpu.get_barrier_semaphore()

    def greet(target):
        pl.semaphore_signal(barrier, inc=1, device_id={"tok": target}, device_id_type=MESH)

    @pl.when(z < Z - 1)
    def _():
        greet(targets[0])

    @pl.when(z > 0)
    def _():
        greet(targets[1])

    greet(targets[2])
    greet(targets[3])

    def copy(direction, zz, xx, p):
        chip = zz * X + xx
        rows = pl.ds(pl.multiple_of(device(zz, xx, c) * shard, shard), shard)
        return pltpu.make_async_remote_copy(
            src_ref=whole.at[p, rows],
            dst_ref=whole.at[p, rows],
            send_sem=send_sem.at[direction, chip, p],
            recv_sem=recv_sem.at[1 if direction == 3 else 0, chip, p],
            device_id={"tok": targets[direction]},
            device_id_type=MESH,
        )

    def from_core(zz, xx, p):
        chip = zz * X + xx
        rows = pl.ds(pl.multiple_of(device(zz, xx, 1 - c) * shard, shard), shard)
        return pltpu.make_async_remote_copy(
            src_ref=whole.at[p, rows],
            dst_ref=whole.at[p, rows],
            send_sem=send_sem.at[3, chip, p],
            recv_sem=recv_sem.at[1, chip, p],
            device_id={"tok": targets[3]},
            device_id_type=MESH,
        )

    def routes(zz, xx, p):
        mine = xx == x
        around = p >= pieces - AROUND
        along = jnp.logical_or(mine, around)
        return (
            along & (zz <= z) & (z < Z - 1),
            along & (zz >= z) & (z > 0),
            mine & jnp.logical_or(zz == z, jnp.logical_not(around)),
        )

    def forward(zz, xx, p):
        for direction, wanted in enumerate(routes(zz, xx, p)):
            @pl.when(wanted)
            def _(direction=direction):
                copy(direction, zz, xx, p).start()
        copy(3, zz, xx, p).start()

    own_rows = pl.ds(pl.multiple_of(me * shard, shard), shard)
    entered = False
    for layer in range(layers):
        for h in range(halves):
            wanted = col_ref[pl.ds(layer, 1), pl.ds(h * HALF, HALF)]
            names = lax.broadcasted_iota(jnp.int32, (bank, HALF), 0)
            pick = jnp.where(names == wanted, 1.0, 0.0).astype(jnp.bfloat16)
            for side, ref in enumerate((qu_ref, qv_ref)):
                p = (layer * halves + h) * 2 + side
                whole[p, own_rows] = jnp.dot(
                    ref[layer], pick, preferred_element_type=jnp.float32
                ).astype(jnp.bfloat16)
                if not entered:
                    pl.semaphore_wait(
                        barrier, 2 + jnp.where(z > 0, 1, 0) + jnp.where(z < Z - 1, 1, 0)
                    )
                    entered = True
                forward(z, x, jnp.int32(p))

    def clear(p, carry):
        acc[p] = jnp.zeros(acc.shape[1:], acc.dtype)
        gram[p] = jnp.zeros(gram.shape[1:], gram.dtype)
        return carry

    lax.fori_loop(0, pieces, clear, 0)
    for load in loads:
        load.wait()

    def use(zz, xx, p):
        from_core(zz, xx, p).wait_recv()
        chip = zz * X + xx
        rows = pl.ds(pl.multiple_of(chip * depth, depth), depth)
        m = (p // (2 * halves)) * 2 + lax.rem(p, 2)
        block = whole[p, rows]
        acc[p] += jnp.dot(toks[m, :, rows], block, preferred_element_type=jnp.float32)
        gram[p] += lax.dot_general(
            block, block, (((0,), (0,)), ((), ())), preferred_element_type=jnp.float32
        )

    def events(t):
        j, p = t // pieces, lax.rem(t, pieces)
        near = (j >= 1) & (j < Z)
        k = j - 1
        end = (z == 0) | (z == Z - 1)
        i = (k - 1) * pieces + p
        mixed = jnp.logical_not(end) & (k >= 1) & (k < Z - 1)
        far = jnp.where(z < 2, k, Z - 1 - k)
        beside = jnp.where(lax.rem(i, 2) == 0, z - 1, z + 1)
        source = jnp.where(k == 0, z, jnp.where(mixed, beside, far))
        piece = jnp.where(mixed, i // 2, p)
        return (
            (near & (z - j >= 0), z - j, x, p),
            (near & (z + j <= Z - 1), z + j, x, p),
            ((j >= 1) & (j <= Z), source, 1 - x, piece),
        )

    def step(t, carry):
        for valid, zz, xx, p in events(t):
            @pl.when(valid)
            def _(zz=zz, xx=xx, p=p):
                copy(2, zz, xx, p).wait_recv()
                forward(zz, xx, p)

        @pl.when(t < 2 * pieces)
        def _():
            use(z, x, t - pieces)

        for valid, zz, xx, p in events(t - 1):
            @pl.when(valid)
            def _(zz=zz, xx=xx, p=p):
                use(zz, xx, p)
        return carry

    lax.fori_loop(pieces, (Z + 1) * pieces + 1, step, 0)

    raw = None
    norm = None
    for h in range(halves):
        spot = lax.broadcasted_iota(jnp.int32, (HALF, out_ref.shape[1]), 0) // RANK
        query = lax.broadcasted_iota(jnp.int32, (HALF, out_ref.shape[1]), 1)
        ones = jnp.where(spot + h * (HALF // RANK) == query, 1.0, 0.0).astype(jnp.bfloat16)
        product = None
        grams = None
        for layer in range(layers):
            p = (layer * halves + h) * 2
            term = acc[p] * acc[p + 1]
            both = gram[p] * gram[p + 1]
            product = term if product is None else product + term
            grams = both if grams is None else grams + both
        down = lax.broadcasted_iota(jnp.int32, (HALF, HALF), 0) // RANK
        across = lax.broadcasted_iota(jnp.int32, (HALF, HALF), 1) // RANK
        column = jnp.sum(jnp.where(down == across, grams, 0.0), axis=0, keepdims=True)
        column = jnp.broadcast_to(column, (8, HALF))
        part = split_dot(product, ones, 2)
        squares = split_dot(column, ones, 3)
        raw = part if raw is None else raw + part
        norm = squares if norm is None else norm + squares
    out_ref[...] = raw * (1.0 / jnp.sqrt(norm[0:1] + 1e-06))

    def drain(n, carry):
        chip, p = n // pieces, lax.rem(n, pieces)
        zz, xx = chip // X, lax.rem(chip, X)
        for direction, wanted in enumerate(routes(zz, xx, p)):
            @pl.when(wanted)
            def _(direction=direction):
                copy(direction, zz, xx, p).wait_send()
        copy(3, zz, xx, p).wait_send()
        return carry

    lax.fori_loop(0, CHIPS * pieces, drain, 0)


def passed_on(activations, gradients, query_u, query_v, block_ids):
    layers, tok_rows, width = activations.shape
    columns = block_ids.shape[1] * WIDTH
    halves = columns // HALF
    pieces = layers * halves * 2
    names = column_names(block_ids)
    flops = 2 * 2 * layers * columns * width * (tok_rows + HALF)
    return pl.pallas_call(
        functools.partial(kernel, layers, halves),
        out_shape=jax.ShapeDtypeStruct((tok_rows, columns // RANK), jnp.float32),
        in_specs=[pl.BlockSpec(memory_space=pl.ANY)] * 2
        + [pl.BlockSpec(memory_space=pltpu.VMEM)] * 3,
        out_specs=pl.BlockSpec(memory_space=pltpu.VMEM),
        scratch_shapes=[
            pltpu.VMEM((pieces, width, HALF), jnp.bfloat16),
            pltpu.VMEM((layers * 2, tok_rows, width), jnp.bfloat16),
            pltpu.VMEM((pieces, tok_rows, HALF), jnp.float32),
            pltpu.VMEM((pieces, HALF, HALF), jnp.float32),
            pltpu.SemaphoreType.DMA((layers * 2,)),
            pltpu.SemaphoreType.DMA((4, CHIPS, pieces)),
            pltpu.SemaphoreType.DMA((2, CHIPS, pieces)),
        ],
        compiler_params=pltpu.CompilerParams(
            collective_id=0, has_side_effects=True, vmem_limit_bytes=56 * 1024 * 1024
        ),
        cost_estimate=pl.CostEstimate(
            flops=flops, bytes_accessed=12 * 1024 * 1024, transcendentals=0
        ),
    )(activations, gradients, query_u, query_v, names)


def per_device(on_grid, activations, gradients, query_u, query_v, block_ids, counts):
    arrange = passed_on if on_grid else gathered
    scaled = arrange(activations, gradients, query_u, query_v, block_ids)
    live = jnp.arange(scaled.shape[0], dtype=jnp.int32) < counts[0]
    return jnp.where(live[:, None], scaled, jnp.zeros_like(scaled))


def solution(mesh):
    placed = (
        P(None, ("groups", "tok"), None),
        P(None, ("groups", "tok"), None),
        P("groups", "tok", None),
        P("groups", "tok", None),
        P("groups", None),
        P(("groups", "tok")),
    )
    return jax.shard_map(
        functools.partial(per_device, mesh.shape["tok"] == CHIPS * CORES),
        mesh=mesh,
        in_specs=placed,
        out_specs=P(("groups", "tok"), None),
        check_vma=False,
    )
```

```python
import functools

import jax
import jax.numpy as jnp
from jax import lax
from jax.experimental import pallas as pl
from jax.experimental.pallas import tpu as pltpu
from jax.sharding import PartitionSpec as P

RANK = 8
QB = 4
WIDTH = QB * RANK
Z = 4
X = 2
CORES = 2
CHIPS = Z * X
HALF = 256
AROUND = 1
MESH = pl.DeviceIdType.MESH


def column_names(block_ids):
    within = jnp.arange(block_ids.shape[1] * WIDTH, dtype=jnp.int32) % WIDTH
    return jnp.repeat(block_ids, WIDTH, axis=1) * WIDTH + within[None, :]


def pick_columns(factor, names):
    rows = jnp.arange(factor.shape[2], dtype=jnp.int32)
    pick = (rows[None, :, None] == names[:, None, :]).astype(factor.dtype)
    chosen = jnp.einsum("lkn,lnc->lkc", factor, pick, preferred_element_type=jnp.float32)
    return chosen.astype(factor.dtype)


def rank_grams(factor):
    per = factor.reshape(factor.shape[0], factor.shape[1], -1, RANK)
    return jnp.einsum("lkqr,lkqs->lqrs", per, per, preferred_element_type=jnp.float32)


def gathered(activations, gradients, query_u, query_v, block_ids):
    layers, tok_rows, _ = activations.shape
    queries = block_ids.shape[1] * QB
    names = column_names(block_ids)
    whole_u = lax.all_gather(pick_columns(query_u, names), "tok", axis=1, tiled=True)
    whole_v = lax.all_gather(pick_columns(query_v, names), "tok", axis=1, tiled=True)
    grad_proj = jnp.einsum("ltk,lkc->ltc", gradients, whole_u, preferred_element_type=jnp.float32)
    act_proj = jnp.einsum("ltk,lkc->ltc", activations, whole_v, preferred_element_type=jnp.float32)
    raw = jnp.sum((grad_proj * act_proj).reshape(layers, tok_rows, queries, RANK), axis=(0, 3))
    norm_sq = jnp.sum(rank_grams(whole_u) * rank_grams(whole_v), axis=(0, 2, 3))
    return (raw / jnp.sqrt(norm_sq + 1e-06)[None, :]).T


def split_dot(value, ones, parts):
    total = None
    for _ in range(parts):
        head = value.astype(jnp.bfloat16)
        term = lax.dot_general(
            ones, head, (((1,), (1,)), ((), ())), preferred_element_type=jnp.float32
        )
        total = term if total is None else total + term
        value = value - head.astype(jnp.float32)
    return total


def kernel(layers, halves, act_ref, grad_ref, qu_ref, qv_ref, col_ref, out_ref,
           whole, toks, acc, gram, tok_sem, send_sem, recv_sem):
    pieces = layers * halves * 2
    shard = qu_ref.shape[1]
    bank = qu_ref.shape[2]
    depth = CORES * shard
    me = lax.axis_index("tok")
    c = lax.rem(me, CORES)
    x = lax.rem(me // CORES, X)
    z = me // (CORES * X)

    def device(zz, xx, cc):
        return (zz * X + xx) * CORES + cc

    targets = (
        device(lax.rem(z + 1, Z), x, c),
        device(lax.rem(z + Z - 1, Z), x, c),
        device(z, 1 - x, c),
        device(z, x, 1 - c),
    )

    loads = []
    for layer in range(layers):
        for side, ref in enumerate((grad_ref, act_ref)):
            m = layer * 2 + side
            loads.append(pltpu.make_async_copy(ref.at[layer], toks.at[m], tok_sem.at[m]))
    for load in loads:
        load.start()

    barrier = pltpu.get_barrier_semaphore()

    def greet(target):
        pl.semaphore_signal(barrier, inc=1, device_id={"tok": target}, device_id_type=MESH)

    @pl.when(z < Z - 1)
    def _():
        greet(targets[0])

    @pl.when(z > 0)
    def _():
        greet(targets[1])

    greet(targets[2])
    greet(targets[3])

    def copy(direction, zz, xx, p):
        chip = zz * X + xx
        rows = pl.ds(pl.multiple_of(device(zz, xx, c) * shard, shard), shard)
        return pltpu.make_async_remote_copy(
            src_ref=whole.at[p, rows],
            dst_ref=whole.at[p, rows],
            send_sem=send_sem.at[direction, chip, p],
            recv_sem=recv_sem.at[1 if direction == 3 else 0, chip, p],
            device_id={"tok": targets[direction]},
            device_id_type=MESH,
        )

    def from_core(zz, xx, p):
        chip = zz * X + xx
        rows = pl.ds(pl.multiple_of(device(zz, xx, 1 - c) * shard, shard), shard)
        return pltpu.make_async_remote_copy(
            src_ref=whole.at[p, rows],
            dst_ref=whole.at[p, rows],
            send_sem=send_sem.at[3, chip, p],
            recv_sem=recv_sem.at[1, chip, p],
            device_id={"tok": targets[3]},
            device_id_type=MESH,
        )

    def routes(zz, xx, p):
        mine = xx == x
        around = p < AROUND
        along = jnp.logical_or(mine, around)
        return (
            along & (zz <= z) & (z < Z - 1),
            along & (zz >= z) & (z > 0),
            mine & jnp.logical_or(zz == z, jnp.logical_not(around)),
        )

    def forward(zz, xx, p):
        for direction, wanted in enumerate(routes(zz, xx, p)):
            @pl.when(wanted)
            def _(direction=direction):
                copy(direction, zz, xx, p).start()
        copy(3, zz, xx, p).start()

    own_rows = pl.ds(pl.multiple_of(me * shard, shard), shard)
    entered = False
    for layer in range(layers):
        for h in range(halves):
            lane = lax.broadcasted_iota(jnp.int32, (1, HALF), 1)
            wanted = lane % WIDTH
            for b in range(HALF // WIDTH):
                start = col_ref[layer, h * (HALF // WIDTH) + b] * WIDTH
                wanted = wanted + jnp.where(lane // WIDTH == b, start, 0)
            names = lax.broadcasted_iota(jnp.int32, (bank, HALF), 0)
            pick = jnp.where(names == wanted, 1.0, 0.0).astype(jnp.bfloat16)
            for side, ref in enumerate((qu_ref, qv_ref)):
                p = (layer * halves + h) * 2 + side
                whole[p, own_rows] = jnp.dot(
                    ref[layer], pick, preferred_element_type=jnp.float32
                ).astype(jnp.bfloat16)
                if not entered:
                    pl.semaphore_wait(
                        barrier, 2 + jnp.where(z > 0, 1, 0) + jnp.where(z < Z - 1, 1, 0)
                    )
                    entered = True
                forward(z, x, jnp.int32(p))

    def clear(p, carry):
        acc[p] = jnp.zeros(acc.shape[1:], acc.dtype)
        gram[p] = jnp.zeros(gram.shape[1:], gram.dtype)
        return carry

    lax.fori_loop(0, pieces, clear, 0)
    for load in loads:
        load.wait()

    def use(zz, xx, p):
        from_core(zz, xx, p).wait_recv()
        chip = zz * X + xx
        rows = pl.ds(pl.multiple_of(chip * depth, depth), depth)
        m = (p // (2 * halves)) * 2 + lax.rem(p, 2)
        block = whole[p, rows]
        acc[p] += jnp.dot(toks[m, :, rows], block, preferred_element_type=jnp.float32)
        gram[p] += lax.dot_general(
            block, block, (((0,), (0,)), ((), ())), preferred_element_type=jnp.float32
        )

    def events(t):
        j, p = t // pieces, lax.rem(t, pieces)
        near = (j >= 1) & (j < Z)
        k = j - 1
        end = (z == 0) | (z == Z - 1)
        i = (k - 1) * pieces + p
        mixed = jnp.logical_not(end) & (k >= 1) & (k < Z - 1)
        far = jnp.where(z < 2, k, Z - 1 - k)
        beside = jnp.where(lax.rem(i, 2) == 0, z - 1, z + 1)
        source = jnp.where(k == 0, z, jnp.where(mixed, beside, far))
        piece = jnp.where(mixed, i // 2, p)
        return (
            (near & (z - j >= 0), z - j, x, p),
            (near & (z + j <= Z - 1), z + j, x, p),
            ((j >= 1) & (j <= Z), source, 1 - x, piece),
        )

    def step(t, carry):
        for valid, zz, xx, p in events(t):
            @pl.when(valid)
            def _(zz=zz, xx=xx, p=p):
                copy(2, zz, xx, p).wait_recv()
                forward(zz, xx, p)

        @pl.when(t < 2 * pieces)
        def _():
            use(z, x, t - pieces)

        for valid, zz, xx, p in events(t - 1):
            @pl.when(valid)
            def _(zz=zz, xx=xx, p=p):
                use(zz, xx, p)
        return carry

    lax.fori_loop(pieces, (Z + 1) * pieces + 1, step, 0)

    raw = None
    norm = None
    for h in range(halves):
        spot = lax.broadcasted_iota(jnp.int32, (out_ref.shape[0], HALF), 1) // RANK
        query = lax.broadcasted_iota(jnp.int32, (out_ref.shape[0], HALF), 0)
        ones = jnp.where(spot + h * (HALF // RANK) == query, 1.0, 0.0).astype(jnp.bfloat16)
        product = None
        grams = None
        for layer in range(layers):
            p = (layer * halves + h) * 2
            term = acc[p] * acc[p + 1]
            both = gram[p] * gram[p + 1]
            product = term if product is None else product + term
            grams = both if grams is None else grams + both
        down = lax.broadcasted_iota(jnp.int32, (HALF, HALF), 0) // RANK
        across = lax.broadcasted_iota(jnp.int32, (HALF, HALF), 1) // RANK
        column = jnp.sum(jnp.where(down == across, grams, 0.0), axis=0, keepdims=True)
        column = jnp.broadcast_to(column, (8, HALF))
        part = split_dot(product, ones, 2)
        squares = split_dot(column, ones, 3)
        raw = part if raw is None else raw + part
        norm = squares if norm is None else norm + squares
    out_ref[...] = raw * (1.0 / jnp.sqrt(norm[:, 0:1] + 1e-06))

    def drain(n, carry):
        chip, p = n // pieces, lax.rem(n, pieces)
        zz, xx = chip // X, lax.rem(chip, X)
        for direction, wanted in enumerate(routes(zz, xx, p)):
            @pl.when(wanted)
            def _(direction=direction):
                copy(direction, zz, xx, p).wait_send()
        copy(3, zz, xx, p).wait_send()
        return carry

    lax.fori_loop(0, CHIPS * pieces, drain, 0)


def passed_on(activations, gradients, query_u, query_v, block_ids):
    layers, tok_rows, width = activations.shape
    columns = block_ids.shape[1] * WIDTH
    halves = columns // HALF
    pieces = layers * halves * 2
    flops = 2 * 2 * layers * columns * width * (tok_rows + HALF)
    return pl.pallas_call(
        functools.partial(kernel, layers, halves),
        out_shape=jax.ShapeDtypeStruct((columns // RANK, tok_rows), jnp.float32),
        in_specs=[pl.BlockSpec(memory_space=pl.ANY)] * 2
        + [pl.BlockSpec(memory_space=pltpu.VMEM)] * 2
        + [pl.BlockSpec(memory_space=pltpu.SMEM)],
        out_specs=pl.BlockSpec(memory_space=pltpu.VMEM),
        scratch_shapes=[
            pltpu.VMEM((pieces, width, HALF), jnp.bfloat16),
            pltpu.VMEM((layers * 2, tok_rows, width), jnp.bfloat16),
            pltpu.VMEM((pieces, tok_rows, HALF), jnp.float32),
            pltpu.VMEM((pieces, HALF, HALF), jnp.float32),
            pltpu.SemaphoreType.DMA((layers * 2,)),
            pltpu.SemaphoreType.DMA((4, CHIPS, pieces)),
            pltpu.SemaphoreType.DMA((2, CHIPS, pieces)),
        ],
        compiler_params=pltpu.CompilerParams(
            collective_id=0, has_side_effects=True, vmem_limit_bytes=56 * 1024 * 1024
        ),
        cost_estimate=pl.CostEstimate(
            flops=flops, bytes_accessed=12 * 1024 * 1024, transcendentals=0
        ),
    )(activations, gradients, query_u, query_v, block_ids)


def per_device(on_grid, activations, gradients, query_u, query_v, block_ids, counts):
    arrange = passed_on if on_grid else gathered
    scaled = arrange(activations, gradients, query_u, query_v, block_ids)
    live = jnp.arange(scaled.shape[1], dtype=jnp.int32) < counts[0]
    return jnp.where(live[None, :], scaled, jnp.zeros_like(scaled)).T


def solution(mesh):
    placed = (
        P(None, ("groups", "tok"), None),
        P(None, ("groups", "tok"), None),
        P("groups", "tok", None),
        P("groups", "tok", None),
        P("groups", None),
        P(("groups", "tok")),
    )
    return jax.shard_map(
        functools.partial(per_device, mesh.shape["tok"] == CHIPS * CORES),
        mesh=mesh,
        in_specs=placed,
        out_specs=P(("groups", "tok"), None),
        check_vma=False,
    )
```
